32 devices in a mesh: groups: 2 (over x), band: 16 (over z, y, core).
Axes of the slice: x: 2, y: 2, z: 4, core: 2. Of those that a mesh axis runs over, the one named last changes fastest.
Arguments:
- grid_state: bfloat16 [8192, 474], P(('groups', 'band')), parts along dimension 0, may hold values from -6 to 6
- mesh_static: float32 [3, 4096], P(None, 'band'), may hold values from -6 to 6
- encoder_senders: int32 [16, 3, 1, 128], P('band'), may hold values from 0 to 255
- encoder_receivers: int32 [16, 3, 1, 128], P('band'), may hold values from 0 to 255
- encoder_counts: int32 [16, 3], P('band'), may hold values from 0 to 128, as said below
- mesh_senders: int32 [256, 128], P('band'), may hold values from 0 to 511
- mesh_receivers: int32 [256, 128], P('band'), may hold values from 0 to 255
- halo_rows: int32 [16, 128], P('band'), may hold values from 0 to 255
- backward_icosa_emitters: int32 [16, 3, 2, 128], P('band'), may hold values from 0 to 255
- backward_cell_destination: int32 [16, 3, 2, 128], P('band'), may hold values from 0 to 255
- backward_active_slot_amounts: int32 [16, 3], P('band'), may hold values from 0 to 256, as said below
- grid_embed: bfloat16 [474, 512], replicated, may hold values from -0.25 to 0.25
- mesh_embed: float32 [3, 512], replicated, may hold values from -3.5 to 3.5
- encoder_source: bfloat16 [512, 512], replicated, may hold values from -0.25 to 0.25
- encoder_target: bfloat16 [512, 512], replicated, may hold values from -0.25 to 0.25
- encoder_message: bfloat16 [512, 512], replicated, may hold values from -0.25 to 0.25
- encoder_retain: bfloat16 [512, 512], replicated, may hold values from -0.25 to 0.25
- encoder_absorb: bfloat16 [512, 512], replicated, may hold values from -0.25 to 0.25
- encoder_finish: bfloat16 [512, 512], replicated, may hold values from -0.25 to 0.25
- process_source: bfloat16 [2, 512, 512], replicated, may hold values from -0.25 to 0.25
- process_target: bfloat16 [2, 512, 512], replicated, may hold values from -0.25 to 0.25
- process_retain: bfloat16 [2, 512, 512], replicated, may hold values from -0.25 to 0.25
- process_absorb: bfloat16 [2, 512, 512], replicated, may hold values from -0.25 to 0.25
- process_finish: bfloat16 [2, 512, 512], replicated, may hold values from -0.25 to 0.25
- decoder_source: bfloat16 [512, 512], replicated, may hold values from -0.25 to 0.25
- decoder_target: bfloat16 [512, 512], replicated, may hold values from -0.25 to 0.25
- decoder_message: bfloat16 [512, 512], replicated, may hold values from -0.25 to 0.25
- decoder_retain: bfloat16 [512, 512], replicated, may hold values from -0.25 to 0.25
- decoder_absorb: bfloat16 [512, 512], replicated, may hold values from -0.25 to 0.25
- readout_matrix: bfloat16 [512, 227], replicated, may hold values from -0.25 to 0.25
Outputs:
- estimated_variables: bfloat16 [8192, 227], P(('groups', 'band')), parts along dimension 0
The draws below stay inside these ranges and needn't reach their ends.
There are 2 independent parts, one for each index of `groups`. The reference program is written for one: setup_inputs(seed, part) draws one part's arguments, and reference() takes and returns one part's arrays. A program takes and returns all parts, laid end to end along the dimension named above; an argument that names none is the same for every part. Nothing has to cross between parts.
Inputs may be any that keep to these rules, and one draw needn't show every extreme that they name: `encoder_counts`: the first count slots of the pair's blocks, in order, are edges; the rest are unused. Pairs with a band or patch outside 0 to 15 have count 0. `backward_active_slot_amounts`: the first count slots of the pair's blocks, in order, are edges; the rest are unused. Pairs with a band or patch outside 0 to 15 have count 0.
All inputs are finite; a program needn't handle non-finite values.
Results may differ from the reference program's by a relative error of at most 0.015.
Values may be sent and summed in bfloat16 or wider, within the bound.
A program may use at most 64 MiB of HBM per device.

```python
import jax
import jax.numpy as jnp
from jax import lax

EMBED_DIM = 512
C_IN = 474
PREDICTED_VARS = 227
FEAT = 3
CELLS_IN_STRIP = 256
M_DEV = 256
EB = 128
LAYERS = 2
STRIP_AMOUNT = 16
HALO = 128
MB_DEV = 16
ENC_BLOCKS = 1
DEC_BLOCKS = 2
POINTS_GLOBE = 4096
NM = 4096
MBLOCKS = 256


def block_counts(seed_key, width):
    row = jnp.arange(STRIP_AMOUNT, dtype=jnp.int32)[:, None]
    column = jnp.arange(3, dtype=jnp.int32)[None, :]
    near_pole = (row < STRIP_AMOUNT // 8) | (row >= STRIP_AMOUNT - STRIP_AMOUNT // 8)
    middle_load = jax.random.randint(seed_key, (STRIP_AMOUNT, 3), width // 2, width + 1)
    counts = jnp.where(near_pole, width, middle_load)
    outside = (row == 0) & (column == 0) | (row == STRIP_AMOUNT - 1) & (column == 2)
    counts = jnp.where(outside, 0, counts)
    return counts.astype(jnp.int32)


def draw_encoder_counts(key, part):
    seed_key = jax.random.fold_in(key, 11)
    return block_counts(seed_key, CELLS_IN_STRIP // 2)


def draw_backward_active_slot_amounts(key, part):
    seed_key = jax.random.fold_in(key, 23)
    return block_counts(seed_key, CELLS_IN_STRIP)


def with_ends(entries, stream_key, low, high):
    longest = entries.shape.index(max(entries.shape))
    spots = []
    for shift in (0, 1):
        where = [jax.random.randint(jax.random.fold_in(stream_key, axis), (), 0, length) for axis, length in enumerate(entries.shape)]
        where[longest] = (where[longest] + shift) % entries.shape[longest]
        spots.append(tuple(where))
    return entries.at[spots[0]].set(low).at[spots[1]].set(high)


def level_of(own_key, extent, cuts, smallest, high):
    loudness = 1.0
    for dim, shards_of in cuts:
        heights = jax.random.uniform(jax.random.fold_in(jax.random.fold_in(own_key, 6), dim), (shards_of,), jnp.float32, smallest / len(cuts), high / len(cuts))
        loudness = loudness * jnp.repeat(jnp.exp(heights), extent[dim] // shards_of).reshape((-1,) + (1,) * (len(extent) - 1 - dim))
    return loudness


def normal_values(key, dims, deviation, bound, shards=(), held_as=jnp.bfloat16):
    array = deviation * jax.random.normal(key, dims, jnp.float32)
    if shards:
        array = array * level_of(key, dims, shards, -0.22, 0.18)
    return jnp.clip(array, -bound, bound).astype(held_as)


def setup_inputs(seed: int = 0, part: int = 0) -> dict:
    seeds = jax.random.split(jax.random.key(seed), 31)
    part_keys = jax.random.split(jax.random.fold_in(seeds[30], part), 31)
    grid_state = normal_values(part_keys[0], (POINTS_GLOBE, C_IN), 1.0, 6.0, ((0, 16),))
    mesh_static = normal_values(seeds[1], (FEAT, NM), 1.0, 6.0, ((1, 16),), jnp.float32)
    encoder_senders = with_ends(jax.random.randint(seeds[2], (STRIP_AMOUNT, 3, ENC_BLOCKS, EB), 0, CELLS_IN_STRIP), jax.random.fold_in(seeds[2], 1), 0, CELLS_IN_STRIP - 1).astype(jnp.int32)
    encoder_receivers = with_ends(jax.random.randint(seeds[3], (STRIP_AMOUNT, 3, ENC_BLOCKS, EB), 0, M_DEV), jax.random.fold_in(seeds[3], 1), 0, M_DEV - 1).astype(jnp.int32)
    encoder_counts = draw_encoder_counts(jax.random.fold_in(seeds[30], 71), part)
    mesh_senders = with_ends(jax.random.randint(seeds[5], (MBLOCKS, EB), 0, M_DEV + 2 * HALO), jax.random.fold_in(seeds[5], 1), 0, (M_DEV + 2 * HALO) - 1).astype(jnp.int32)
    mesh_receivers = with_ends(jax.random.randint(seeds[6], (MBLOCKS, EB), 0, M_DEV), jax.random.fold_in(seeds[6], 1), 0, M_DEV - 1).astype(jnp.int32)
    halo_rows = with_ends(jax.random.randint(seeds[7], (STRIP_AMOUNT, HALO), 0, M_DEV), jax.random.fold_in(seeds[7], 1), 0, M_DEV - 1).astype(jnp.int32)
    backward_icosa_emitters = with_ends(jax.random.randint(seeds[8], (STRIP_AMOUNT, 3, DEC_BLOCKS, EB), 0, M_DEV), jax.random.fold_in(seeds[8], 1), 0, M_DEV - 1).astype(jnp.int32)
    backward_cell_destination = with_ends(jax.random.randint(seeds[9], (STRIP_AMOUNT, 3, DEC_BLOCKS, EB), 0, CELLS_IN_STRIP), jax.random.fold_in(seeds[9], 1), 0, CELLS_IN_STRIP - 1).astype(jnp.int32)
    backward_active_slot_amounts = draw_backward_active_slot_amounts(jax.random.fold_in(seeds[30], 71), part)
    grid_embed = normal_values(seeds[11], (C_IN, EMBED_DIM), C_IN ** -0.5, 0.25)
    mesh_embed = normal_values(seeds[12], (FEAT, EMBED_DIM), FEAT ** -0.5, 3.5, (), jnp.float32)
    encoder_source = normal_values(seeds[13], (EMBED_DIM, EMBED_DIM), EMBED_DIM ** -0.5, 0.25)
    encoder_target = normal_values(seeds[14], (EMBED_DIM, EMBED_DIM), EMBED_DIM ** -0.5, 0.25)
    encoder_message = normal_values(seeds[15], (EMBED_DIM, EMBED_DIM), EMBED_DIM ** -0.5, 0.25)
    encoder_retain = normal_values(seeds[16], (EMBED_DIM, EMBED_DIM), EMBED_DIM ** -0.5, 0.25)
    encoder_absorb = normal_values(seeds[17], (EMBED_DIM, EMBED_DIM), EMBED_DIM ** -0.5, 0.25)
    encoder_finish = normal_values(seeds[18], (EMBED_DIM, EMBED_DIM), EMBED_DIM ** -0.5, 0.25)
    process_source = normal_values(seeds[19], (LAYERS, EMBED_DIM, EMBED_DIM), EMBED_DIM ** -0.5, 0.25)
    process_target = normal_values(seeds[20], (LAYERS, EMBED_DIM, EMBED_DIM), EMBED_DIM ** -0.5, 0.25)
    process_retain = normal_values(seeds[21], (LAYERS, EMBED_DIM, EMBED_DIM), EMBED_DIM ** -0.5, 0.25)
    process_absorb = normal_values(seeds[22], (LAYERS, EMBED_DIM, EMBED_DIM), EMBED_DIM ** -0.5, 0.25)
    process_finish = normal_values(seeds[23], (LAYERS, EMBED_DIM, EMBED_DIM), EMBED_DIM ** -0.5, 0.25)
    decoder_source = normal_values(seeds[24], (EMBED_DIM, EMBED_DIM), EMBED_DIM ** -0.5, 0.25)
    decoder_target = normal_values(seeds[25], (EMBED_DIM, EMBED_DIM), EMBED_DIM ** -0.5, 0.25)
    decoder_message = normal_values(seeds[26], (EMBED_DIM, EMBED_DIM), EMBED_DIM ** -0.5, 0.25)
    decoder_retain = normal_values(seeds[27], (EMBED_DIM, EMBED_DIM), EMBED_DIM ** -0.5, 0.25)
    decoder_absorb = normal_values(seeds[28], (EMBED_DIM, EMBED_DIM), EMBED_DIM ** -0.5, 0.25)
    readout_matrix = normal_values(seeds[29], (EMBED_DIM, PREDICTED_VARS), EMBED_DIM ** -0.5, 0.25)
    return dict(grid_state=grid_state, mesh_static=mesh_static, encoder_senders=encoder_senders, encoder_receivers=encoder_receivers, encoder_counts=encoder_counts, mesh_senders=mesh_senders, mesh_receivers=mesh_receivers, halo_rows=halo_rows, backward_icosa_emitters=backward_icosa_emitters, backward_cell_destination=backward_cell_destination, backward_active_slot_amounts=backward_active_slot_amounts, grid_embed=grid_embed, mesh_embed=mesh_embed, encoder_source=encoder_source, encoder_target=encoder_target, encoder_message=encoder_message, encoder_retain=encoder_retain, encoder_absorb=encoder_absorb, encoder_finish=encoder_finish, process_source=process_source, process_target=process_target, process_retain=process_retain, process_absorb=process_absorb, process_finish=process_finish, decoder_source=decoder_source, decoder_target=decoder_target, decoder_message=decoder_message, decoder_retain=decoder_retain, decoder_absorb=decoder_absorb, readout_matrix=readout_matrix)


def product(left, right):
    return jnp.dot(left, right, preferred_element_type=jnp.float32)

def norm_rows(values):
    centre = values - lax.optimization_barrier(jnp.mean(values, axis=-1, keepdims=True))
    spread = lax.optimization_barrier(jnp.mean(centre * centre, axis=-1, keepdims=True))
    return centre * lax.rsqrt(spread + 1e-05)

def edge_messages(rows, receivers, counts, target, weight, node_count):
    width = rows.shape[1]
    flat_in = receivers.reshape(-1)
    joined = rows.reshape(-1, rows.shape[-1]).astype(jnp.float32) + jnp.take(target, flat_in, axis=0)
    hidden = jax.nn.silu(joined).astype(jnp.bfloat16)
    message = product(hidden, weight)
    live_slots = jnp.arange(width, dtype=jnp.int32)[None, :] < counts[:, None]
    message = jnp.where(live_slots.reshape(-1, 1), message, 0.0)
    return jax.ops.segment_sum(message, flat_in, num_segments=node_count).astype(jnp.bfloat16)

def mesh_sum(table, senders, receivers, target, node_count):
    flat_in = receivers.reshape(-1)
    joined = jnp.take(table, senders.reshape(-1), axis=0).astype(jnp.float32) + jnp.take(target, flat_in, axis=0)
    return jax.ops.segment_sum(jax.nn.silu(joined), flat_in, num_segments=node_count).astype(jnp.bfloat16)

def vertex_refresh(state, coarse_vertex_values, gathered, w_self, w_incoming, w_finish):
    inner_rows = jax.nn.silu(product(coarse_vertex_values, w_self) + product(gathered, w_incoming)).astype(jnp.bfloat16)
    return state + norm_rows(product(inner_rows, w_finish))

def reference(grid_state, mesh_static, encoder_senders, encoder_receivers, encoder_counts, mesh_senders, mesh_receivers, halo_rows, backward_icosa_emitters, backward_cell_destination, backward_active_slot_amounts, grid_embed, mesh_embed, encoder_source, encoder_target, encoder_message, encoder_retain, encoder_absorb, encoder_finish, process_source, process_target, process_retain, process_absorb, process_finish, decoder_source, decoder_target, decoder_message, decoder_retain, decoder_absorb, readout_matrix):
    sender_index = jnp.arange(STRIP_AMOUNT, dtype=jnp.int32)[:, None]
    offsets = jnp.arange(3, dtype=jnp.int32)[None, :]
    emitter_region_strip = jnp.clip(sender_index + offsets - 1, 0, STRIP_AMOUNT - 1).astype(jnp.int32)
    cell_hidden_state = norm_rows(jax.nn.silu(product(grid_state, grid_embed))).astype(jnp.bfloat16)
    grid_source = product(cell_hidden_state, encoder_source).astype(jnp.bfloat16).reshape(STRIP_AMOUNT, CELLS_IN_STRIP, EMBED_DIM)
    mesh_state = jax.nn.silu(jnp.dot(mesh_static.T, mesh_embed, precision=lax.Precision.HIGHEST))
    mesh_low = mesh_state.astype(jnp.bfloat16)
    mesh_target = product(mesh_low, encoder_target).reshape(STRIP_AMOUNT, M_DEV, EMBED_DIM)
    encoder_ids = encoder_senders[emitter_region_strip, 2 - offsets]

    def encode_one(inputs):
        bands, ids, receivers, counts, target = inputs
        rows = grid_source[bands[:, None, None], ids].reshape(3, -1, EMBED_DIM)
        return edge_messages(rows, receivers, counts, target, encoder_message, M_DEV)
    gathered = lax.map(encode_one, (emitter_region_strip, encoder_ids, encoder_receivers, encoder_counts, mesh_target))
    mesh_state = vertex_refresh(mesh_state, mesh_low, gathered.reshape(NM, EMBED_DIM), encoder_retain, encoder_absorb, encoder_finish)
    block_senders = mesh_senders.reshape(STRIP_AMOUNT, MB_DEV, EB)
    block_receivers = mesh_receivers.reshape(STRIP_AMOUNT, MB_DEV, EB)

    def patch_sum(table, senders, receivers, target):
        return mesh_sum(table, senders, receivers, target, M_DEV)
    for layer_index in range(LAYERS):
        mesh_low = mesh_state.astype(jnp.bfloat16)
        source_rows = product(mesh_low, process_source[layer_index]).astype(jnp.bfloat16).reshape(STRIP_AMOUNT, M_DEV, EMBED_DIM)
        target_rows = product(mesh_low, process_target[layer_index]).reshape(STRIP_AMOUNT, M_DEV, EMBED_DIM)
        rim_rows = source_rows[sender_index, halo_rows]
        blank_rim = jnp.zeros((1, HALO, EMBED_DIM), jnp.bfloat16)
        below = jnp.concatenate([blank_rim, rim_rows[:-1]], axis=0)
        above = jnp.concatenate([rim_rows[1:], blank_rim], axis=0)
        extended = jnp.concatenate([below, source_rows, above], axis=1)
        gathered = jax.vmap(patch_sum)(extended, block_senders, block_receivers, target_rows)
        mesh_state = vertex_refresh(mesh_state, mesh_low, gathered.reshape(NM, EMBED_DIM), process_retain[layer_index], process_absorb[layer_index], process_finish[layer_index])
    mesh_low = mesh_state.astype(jnp.bfloat16)
    mesh_source = product(mesh_low, decoder_source).astype(jnp.bfloat16).reshape(STRIP_AMOUNT, M_DEV, EMBED_DIM)
    cell_destination_state = product(cell_hidden_state, decoder_target).reshape(STRIP_AMOUNT, CELLS_IN_STRIP, EMBED_DIM)

    def unpack_strip_cells(inputs):
        bands, ids, receivers, counts, target, latent = inputs
        rows = mesh_source[bands[:, None, None], ids].reshape(3, -1, EMBED_DIM)
        summed = edge_messages(rows, receivers, counts, target, decoder_message, CELLS_IN_STRIP)
        inner_rows = jax.nn.silu(product(latent, decoder_retain) + product(summed, decoder_absorb)).astype(jnp.bfloat16)
        return product(inner_rows, readout_matrix).astype(jnp.bfloat16)
    estimated_variables = lax.map(unpack_strip_cells, (emitter_region_strip, backward_icosa_emitters, backward_cell_destination, backward_active_slot_amounts, cell_destination_state, cell_hidden_state.reshape(STRIP_AMOUNT, CELLS_IN_STRIP, EMBED_DIM)))
    return estimated_variables.reshape(POINTS_GLOBE, PREDICTED_VARS)
```

```python
import functools

import jax
import jax.numpy as jnp
from jax import lax
from jax.experimental import pallas as pl
from jax.experimental.pallas import tpu as pltpu
from jax.sharding import PartitionSpec as P

MESH = pl.DeviceIdType.MESH
BF = jnp.bfloat16
F32 = jnp.float32
LANES = 128


def product(left, right):
    return jnp.dot(left, right, preferred_element_type=F32)


def product_nt(left, right):
    return lax.dot_general(left, right, (((1,), (1,)), ((), ())), preferred_element_type=F32)


def product_tn(left, right):
    return lax.dot_general(left, right, (((0,), (0,)), ((), ())), preferred_element_type=F32)


def silu(x):
    half = 0.5 * x
    return half + half * jnp.tanh(half)


def norm_rows(values):
    centre = values - jnp.mean(values, axis=-1, keepdims=True)
    spread = jnp.mean(centre * centre, axis=-1, keepdims=True)
    return centre * lax.rsqrt(spread + 1e-05)


def hot_columns(column, width):
    ids = lax.broadcasted_iota(jnp.int32, (column.shape[0], width), 1).astype(F32)
    return jnp.where(column == ids, 1.0, 0.0).astype(BF)


def hot_rows(row, height):
    ids = lax.broadcasted_iota(jnp.int32, (height, row.shape[1]), 0).astype(F32)
    return jnp.where(row == ids, 1.0, 0.0).astype(BF)


def kernel(
    n,
    state_t,
    static,
    enc_send,
    enc_recv,
    enc_counts,
    mesh_send,
    mesh_recv,
    halo,
    dec_send,
    dec_recv,
    dec_counts,
    grid_embed,
    mesh_embed,
    readout_t,
    w_es,
    w_et,
    w_em,
    w_er,
    w_ea,
    w_ef,
    w_ps,
    w_pt,
    w_pr,
    w_pa,
    w_pf,
    w_ds,
    w_dt,
    w_dm,
    w_dr,
    w_da,
    out,
    weights,
    id_rows,
    id_cols,
    enc_leave,
    enc_table,
    rim,
    tables,
    dec_table,
    grid_tgt,
    hot_mesh,
    sel_mesh,
    hot_dec,
    sel_dec,
    hidden,
    weight_sem,
    send_sem,
    recv_sem,
):
    layers = w_ps.shape[0]
    nodes = static.shape[1]
    cells = state_t.shape[1]
    width_e = enc_send.shape[2] * LANES
    blocks_d = dec_send.shape[2]
    width_d = blocks_d * LANES
    rim_w = halo.shape[1]
    blocks_m = mesh_send.shape[0]
    ext_w = nodes + 2 * rim_w

    me = lax.axis_index("band")
    left = lax.rem(me + n - 1, n)
    right = lax.rem(me + 1, n)
    has_left = me > 0
    has_right = me < n - 1

    barrier = pltpu.get_barrier_semaphore()

    @pl.when(has_left)
    def _():
        pl.semaphore_signal(barrier, inc=1, device_id={"band": left}, device_id_type=MESH)

    @pl.when(has_right)
    def _():
        pl.semaphore_signal(barrier, inc=1, device_id={"band": right}, device_id_type=MESH)

    order = [w_es, w_et, w_er, w_em, w_ea, w_ef]
    names = ["es", "et", "er", "em", "ea", "ef"]
    for l in range(layers):
        order += [w.at[l] for w in (w_ps, w_pt, w_pr, w_pa, w_pf)]
        names += [a + str(l) for a in ("ps", "pt", "pr", "pa", "pf")]
    order += [w_ds, w_dt, w_dr, w_dm, w_da]
    names += ["ds", "dt", "dr", "dm", "da"]
    copies = {}
    for k, (name, ref) in enumerate(zip(names, order)):
        copy = pltpu.make_async_copy(ref, weights.at[k], weight_sem.at[k])
        copy.start()
        copies[name] = (copy, k)

    def weight(name):
        copy, k = copies[name]
        copy.wait()
        return weights[k]

    def to_left(r, src, dst):
        return pltpu.make_async_remote_copy(
            src_ref=src, dst_ref=dst, send_sem=send_sem.at[2 * r], recv_sem=recv_sem.at[2 * r],
            device_id={"band": left}, device_id_type=MESH)

    def to_right(r, src, dst):
        return pltpu.make_async_remote_copy(
            src_ref=src, dst_ref=dst, send_sem=send_sem.at[2 * r + 1],
            recv_sem=recv_sem.at[2 * r + 1], device_id={"band": right}, device_id_type=MESH)

    sent = []

    def exchange(r, src_left, src_right, low, high):
        one, two = to_left(r, src_left, high), to_right(r, src_right, low)

        @pl.when(has_left)
        def _():
            one.start()

        @pl.when(has_right)
        def _():
            two.start()

        sent.append((one, two))

    def arrive(r):
        one, two = sent[r]

        @pl.when(has_left)
        def _():
            two.wait_recv()

        @pl.when(has_right)
        def _():
            one.wait_recv()

    lows = [enc_table.at[0]]
    highs = [enc_table.at[2]]
    for l in range(layers):
        lows.append(tables.at[l, pl.ds(0, rim_w)])
        highs.append(tables.at[l, pl.ds(rim_w + nodes, rim_w)])
    lows.append(dec_table.at[0])
    highs.append(dec_table.at[2])

    @pl.when(jnp.logical_not(has_left))
    def _():
        for ref in lows:
            ref[...] = jnp.zeros(ref.shape, BF)

    @pl.when(jnp.logical_not(has_right))
    def _():
        for ref in highs:
            ref[...] = jnp.zeros(ref.shape, BF)

    id_rows[...] = jnp.zeros(id_rows.shape, F32)
    base_ms, base_mr = 0, blocks_m
    base_h = 2 * blocks_m
    base_es = base_h + 8
    base_er = base_es + 8
    base_ds = base_er + 8
    base_dr = base_ds + 8
    id_rows[base_ms:base_ms + blocks_m, :] = mesh_send[...].astype(F32)
    id_rows[base_mr:base_mr + blocks_m, :] = mesh_recv[...].astype(F32)
    id_rows[base_h:base_h + 1, :] = halo[...].astype(F32)
    for o in range(3):
        id_rows[base_es + o:base_es + o + 1, :] = enc_send[0, o].astype(F32)
        id_rows[base_er + o:base_er + o + 1, :] = enc_recv[0, o].astype(F32)
        id_rows[base_ds + 2 * o:base_ds + 2 * o + 2, :] = dec_send[0, o].astype(F32)
        id_rows[base_dr + 2 * o:base_dr + 2 * o + 2, :] = dec_recv[0, o].astype(F32)
    id_cols[...] = id_rows[...].T

    def column(j):
        return id_cols[:, j:j + 1]

    latent = norm_rows(silu(product_tn(state_t[...], grid_embed[...]))).astype(BF)
    grid_source = product(latent, weight("es")).astype(BF)
    for o in range(3):
        rows = product(hot_columns(column(base_es + o), cells), grid_source).astype(BF)
        if o == 1:
            enc_table[1] = rows
        else:
            enc_leave[o // 2] = rows
    pl.semaphore_wait(barrier, has_left.astype(jnp.int32) + has_right.astype(jnp.int32))
    exchange(0, enc_leave.at[0], enc_leave.at[1], enc_table.at[0], enc_table.at[2])

    static_t = jnp.concatenate([static[...], jnp.zeros((5, nodes), F32)], axis=0).T
    total = static_t[:, 0:1] * mesh_embed[0:1, :]
    for f in range(1, static.shape[0]):
        total = total + static_t[:, f:f + 1] * mesh_embed[f:f + 1, :]
    mesh_state = silu(total)
    mesh_low = mesh_state.astype(BF)
    target = product(mesh_low, weight("et")).astype(BF)
    kept = product(mesh_low, weight("er"))
    sel = []
    lane = lax.broadcasted_iota(jnp.int32, (1, LANES), 1)
    for o in range(3):
        live = lane < enc_counts[0, o]
        sel.append(hot_rows(jnp.where(live, id_rows[base_er + o:base_er + o + 1, :], -1.0), nodes))

    hot_halo = hot_columns(column(base_h), nodes)
    for j in range(blocks_m):
        at = slice(j * LANES, (j + 1) * LANES)
        hot_mesh[at, 0:ext_w] = hot_columns(column(base_ms + j), ext_w)
        hot_mesh[at, ext_w:ext_w + nodes] = hot_columns(column(base_mr + j), nodes)
        sel_mesh[:, at] = hot_rows(id_rows[base_mr + j:base_mr + j + 1, :], nodes)
    for o in range(3):
        for b in range(blocks_d):
            j = o * blocks_d + b
            at = slice(j * LANES, (j + 1) * LANES)
            hot_dec[at, 0:nodes] = hot_columns(column(base_ds + j), nodes)
            hot_dec[at, nodes:nodes + cells] = hot_columns(column(base_dr + j), cells)
            live = lane + b * LANES < dec_counts[0, o]
            row = jnp.where(live, id_rows[base_dr + j:base_dr + j + 1, :], -1.0)
            sel_dec[:, at] = hot_rows(row, cells)

    arrive(0)
    for o in range(3):
        joined = enc_table[o].astype(F32) + product(hot_columns(column(base_er + o), nodes), target)
        hidden[o * width_e:(o + 1) * width_e, :] = silu(joined).astype(BF)
    summed = product(jnp.concatenate(sel, axis=1), hidden[0:3 * width_e, :]).astype(BF)
    summed = product(summed, weight("em")).astype(BF)
    inner = silu(kept + product(summed, weight("ea"))).astype(BF)
    mesh_state = mesh_state + norm_rows(product(inner, weight("ef")))

    chunk = 512
    for l in range(layers):
        tag = str(l)
        mesh_low = mesh_state.astype(BF)
        source = product(mesh_low, weight("ps" + tag)).astype(BF)
        rim[l] = product(hot_halo, source).astype(BF)
        exchange(1 + l, rim.at[l], rim.at[l], lows[1 + l], highs[1 + l])
        tables[l, rim_w:rim_w + nodes, :] = source
        tables[l, ext_w:ext_w + nodes, :] = product(mesh_low, weight("pt" + tag)).astype(BF)
        kept = product(mesh_low, weight("pr" + tag))
        if l == 0:
            grid_tgt[...] = product(latent, weight("dt")).astype(BF)
            grid_kept = product(latent, weight("dr"))
        arrive(1 + l)
        for c in range(blocks_m * LANES // chunk):
            at = slice(c * chunk, (c + 1) * chunk)
            hidden[at, :] = silu(product(hot_mesh[at, :], tables[l])).astype(BF)
        summed = product(sel_mesh[...], hidden[...]).astype(BF)
        inner = silu(kept + product(summed, weight("pa" + tag))).astype(BF)
        mesh_state = mesh_state + norm_rows(product(inner, weight("pf" + tag)))

    dec_table[1] = product(mesh_state.astype(BF), weight("ds")).astype(BF)
    exchange(1 + layers, dec_table.at[1], dec_table.at[1], dec_table.at[0], dec_table.at[2])

    def decode(o):
        at = slice(o * width_d, (o + 1) * width_d)
        joined = product(hot_dec[at, 0:nodes], dec_table[o]) + product(
            hot_dec[at, nodes:nodes + cells], grid_tgt[...])
        hidden[at, :] = silu(joined).astype(BF)

    decode(1)
    arrive(1 + layers)
    decode(0)
    decode(2)
    summed = product(sel_dec[...], hidden[0:3 * width_d, :]).astype(BF)
    summed = product(summed, weight("dm")).astype(BF)
    inner = silu(grid_kept + product(summed, weight("da"))).astype(BF)
    out[...] = product_nt(readout_t[...], inner).astype(BF)

    for one, two in sent:
        @pl.when(has_left)
        def _(one=one):
            one.wait_send()

        @pl.when(has_right)
        def _(two=two):
            two.wait_send()


def body(
    n,
    grid_state,
    mesh_static,
    encoder_senders,
    encoder_receivers,
    encoder_counts,
    mesh_senders,
    mesh_receivers,
    halo_rows,
    backward_icosa_emitters,
    backward_cell_destination,
    backward_active_slot_amounts,
    grid_embed,
    mesh_embed,
    encoder_source,
    encoder_target,
    encoder_message,
    encoder_retain,
    encoder_absorb,
    encoder_finish,
    process_source,
    process_target,
    process_retain,
    process_absorb,
    process_finish,
    decoder_source,
    decoder_target,
    decoder_message,
    decoder_retain,
    decoder_absorb,
    readout_matrix,
):
    cells = grid_state.shape[0]
    nodes = mesh_static.shape[1]
    dim = grid_embed.shape[1]
    layers = process_source.shape[0]
    rim_w = halo_rows.shape[1]
    edges = mesh_senders.size
    width_e = encoder_senders.size // 3
    width_d = backward_icosa_emitters.size // 3
    n_weights = 11 + 5 * layers
    rounds = 2 + layers
    vmem = pl.BlockSpec(memory_space=pltpu.VMEM)
    smem = pl.BlockSpec(memory_space=pltpu.SMEM)
    far = pl.BlockSpec(memory_space=pl.ANY)
    out_t = pl.pallas_call(
        functools.partial(kernel, n),
        out_shape=jax.ShapeDtypeStruct((readout_matrix.shape[1], cells), BF),
        in_specs=[vmem] * 4 + [smem] + [vmem] * 5 + [smem] + [vmem] * 3 + [far] * 16,
        out_specs=vmem,
        scratch_shapes=[
            pltpu.VMEM((n_weights, dim, dim), BF),
            pltpu.VMEM((LANES, LANES), F32),
            pltpu.VMEM((LANES, LANES), F32),
            pltpu.VMEM((2, width_e, dim), BF),
            pltpu.VMEM((3, width_e, dim), BF),
            pltpu.VMEM((layers, rim_w, dim), BF),
            pltpu.VMEM((layers, 2 * rim_w + 2 * nodes, dim), BF),
            pltpu.VMEM((3, nodes, dim), BF),
            pltpu.VMEM((cells, dim), BF),
            pltpu.VMEM((edges, 2 * rim_w + 2 * nodes), BF),
            pltpu.VMEM((nodes, edges), BF),
            pltpu.VMEM((3 * width_d, nodes + cells), BF),
            pltpu.VMEM((cells, 3 * width_d), BF),
            pltpu.VMEM((edges, dim), BF),
            pltpu.SemaphoreType.DMA((n_weights,)),
            pltpu.SemaphoreType.DMA((2 * rounds,)),
            pltpu.SemaphoreType.DMA((2 * rounds,)),
        ],
        compiler_params=pltpu.CompilerParams(
            collective_id=0, has_side_effects=True, vmem_limit_bytes=56 * 1024 * 1024
        ),
    )(
        grid_state.T,
        mesh_static,
        encoder_senders,
        encoder_receivers,
        encoder_counts,
        mesh_senders,
        mesh_receivers,
        halo_rows,
        backward_icosa_emitters,
        backward_cell_destination,
        backward_active_slot_amounts,
        grid_embed,
        mesh_embed,
        readout_matrix.T,
        encoder_source,
        encoder_target,
        encoder_message,
        encoder_retain,
        encoder_absorb,
        encoder_finish,
        process_source,
        process_target,
        process_retain,
        process_absorb,
        process_finish,
        decoder_source,
        decoder_target,
        decoder_message,
        decoder_retain,
        decoder_absorb,
    )
    return out_t.T


def solution(mesh):
    placed = (
        P(("groups", "band"), None),
        P(None, "band"),
        P("band", None, None, None),
        P("band", None, None, None),
        P("band", None),
        P("band", None),
        P("band", None),
        P("band", None),
        P("band", None, None, None),
        P("band", None, None, None),
        P("band", None),
    ) + (P(),) * 19
    return jax.shard_map(
        functools.partial(body, mesh.shape["band"]),
        mesh=mesh,
        in_specs=placed,
        out_specs=P(("groups", "band"), None),
        check_vma=False,
    )
```

```python
import functools

import jax
import jax.numpy as jnp
from jax import lax
from jax.experimental import pallas as pl
from jax.experimental.pallas import tpu as pltpu
from jax.sharding import PartitionSpec as P

MESH = pl.DeviceIdType.MESH
BF = jnp.bfloat16
F32 = jnp.float32
LANES = 128


def product(left, right):
    return jnp.dot(left, right, preferred_element_type=F32)


def product_nt(left, right):
    return lax.dot_general(left, right, (((1,), (1,)), ((), ())), preferred_element_type=F32)


def product_tn(left, right):
    return lax.dot_general(left, right, (((0,), (0,)), ((), ())), preferred_element_type=F32)


def silu(x):
    half = 0.5 * x
    return half + half * jnp.tanh(half)


def norm_rows(values):
    centre = values - jnp.mean(values, axis=-1, keepdims=True)
    spread = jnp.mean(centre * centre, axis=-1, keepdims=True)
    return centre * lax.rsqrt(spread + 1e-05)


def hot_columns(column, width, first=0):
    ids = (lax.broadcasted_iota(jnp.int32, (column.shape[0], width), 1) + first).astype(F32)
    return jnp.where(column == ids, 1.0, 0.0).astype(BF)


def hot_rows(row, height):
    ids = lax.broadcasted_iota(jnp.int32, (height, row.shape[1]), 0).astype(F32)
    return jnp.where(row == ids, 1.0, 0.0).astype(BF)


def kernel(
    n,
    state_t,
    static,
    enc_send,
    enc_recv,
    enc_counts,
    mesh_send,
    mesh_recv,
    halo,
    dec_send,
    dec_recv,
    dec_counts,
    grid_embed,
    mesh_embed,
    readout_t,
    w_es,
    w_et,
    w_em,
    w_er,
    w_ea,
    w_ef,
    w_ps,
    w_pt,
    w_pr,
    w_pa,
    w_pf,
    w_ds,
    w_dt,
    w_dm,
    w_dr,
    w_da,
    out,
    weights,
    id_rows,
    id_cols,
    enc_leave,
    enc_table,
    pre_enc,
    rim,
    rim_table,
    own_table,
    pre_mesh,
    dec_table,
    pre_dec,
    grid_tgt,
    hot_mesh,
    sel_mesh,
    hot_dec,
    sel_dec,
    hidden,
    weight_sem,
    send_sem,
    recv_sem,
):
    layers = w_ps.shape[0]
    nodes = static.shape[1]
    cells = state_t.shape[1]
    width_e = enc_send.shape[2] * LANES
    blocks_d = dec_send.shape[2]
    width_d = blocks_d * LANES
    rim_w = halo.shape[1]
    blocks_m = mesh_send.shape[0]
    ext_w = nodes + 2 * rim_w

    me = lax.axis_index("band")
    left = lax.rem(me + n - 1, n)
    right = lax.rem(me + 1, n)
    has_left = me > 0
    has_right = me < n - 1

    barrier = pltpu.get_barrier_semaphore()

    @pl.when(has_left)
    def _():
        pl.semaphore_signal(barrier, inc=1, device_id={"band": left}, device_id_type=MESH)

    @pl.when(has_right)
    def _():
        pl.semaphore_signal(barrier, inc=1, device_id={"band": right}, device_id_type=MESH)

    order = [w_es, w_et, w_em, w_ea, w_er, w_ef]
    names = ["es", "et", "em", "ea", "er", "ef"]
    for l in range(layers):
        order += [w.at[l] for w in (w_ps, w_pt, w_pr, w_pa, w_pf)]
        names += [a + str(l) for a in ("ps", "pt", "pr", "pa", "pf")]
    order += [w_ds, w_dt, w_dr, w_dm, w_da]
    names += ["ds", "dt", "dr", "dm", "da"]
    copies = {}
    for k, (name, ref) in enumerate(zip(names, order)):
        copy = pltpu.make_async_copy(ref, weights.at[k], weight_sem.at[k])
        copy.start()
        copies[name] = (copy, k)

    def weight(name):
        copy, k = copies[name]
        copy.wait()
        return weights[k]

    dim = weights.shape[-1]
    half = dim // 2
    cols = [slice(0, half), slice(half, dim)]

    def to_side(k, src, dst, side):
        return pltpu.make_async_remote_copy(
            src_ref=src, dst_ref=dst, send_sem=send_sem.at[k], recv_sem=recv_sem.at[k],
            device_id={"band": side}, device_id_type=MESH)

    lows, highs = {}, {}
    for h in range(2):
        lows[0, h], highs[0, h] = enc_table.at[h, 0], enc_table.at[h, 1]
        for l in range(layers):
            lows[1 + l, h] = rim_table.at[l, h, pl.ds(0, rim_w)]
            highs[1 + l, h] = rim_table.at[l, h, pl.ds(rim_w, rim_w)]
        lows[1 + layers, h], highs[1 + layers, h] = dec_table.at[h, 0], dec_table.at[h, 1]

    sent = {}

    def exchange(r, h, src_left, src_right):
        k = 2 * (2 * r + h)
        one = to_side(k, src_left, highs[r, h], left)
        two = to_side(k + 1, src_right, lows[r, h], right)

        @pl.when(has_left)
        def _():
            one.start()

        @pl.when(has_right)
        def _():
            two.start()

        sent[r, h] = (one, two)

    def arrive(r, h):
        one, two = sent[r, h]

        @pl.when(has_left)
        def _():
            two.wait_recv()

        @pl.when(has_right)
        def _():
            one.wait_recv()

    @pl.when(jnp.logical_not(has_left))
    def _():
        for ref in lows.values():
            ref[...] = jnp.zeros(ref.shape, BF)

    @pl.when(jnp.logical_not(has_right))
    def _():
        for ref in highs.values():
            ref[...] = jnp.zeros(ref.shape, BF)

    id_rows[...] = jnp.zeros(id_rows.shape, F32)
    base_ms, base_mr = 0, blocks_m
    base_h = 2 * blocks_m
    base_es = base_h + 8
    base_er = base_es + 8
    base_ds = base_er + 8
    base_dr = base_ds + 8
    id_rows[base_ms:base_ms + blocks_m, :] = mesh_send[...].astype(F32)
    id_rows[base_mr:base_mr + blocks_m, :] = mesh_recv[...].astype(F32)
    id_rows[base_h:base_h + 1, :] = halo[...].astype(F32)
    for o in range(3):
        id_rows[base_es + o:base_es + o + 1, :] = enc_send[0, o].astype(F32)
        id_rows[base_er + o:base_er + o + 1, :] = enc_recv[0, o].astype(F32)
        id_rows[base_ds + 2 * o:base_ds + 2 * o + 2, :] = dec_send[0, o].astype(F32)
        id_rows[base_dr + 2 * o:base_dr + 2 * o + 2, :] = dec_recv[0, o].astype(F32)
    id_cols[...] = id_rows[...].T

    def column(j):
        return id_cols[:, j:j + 1]

    latent = norm_rows(silu(product_tn(state_t[...], grid_embed[...]))).astype(BF)
    w = weight("es")
    hot_left = hot_columns(column(base_es), cells)
    hot_right = hot_columns(column(base_es + 2), cells)
    hot_own = hot_columns(column(base_es + 1), cells)
    grid_source = []
    for h in range(2):
        grid_source.append(product(latent, w[:, cols[h]]).astype(BF))
        enc_leave[h, 0] = product(hot_left, grid_source[h]).astype(BF)
        enc_leave[h, 1] = product(hot_right, grid_source[h]).astype(BF)
        if h == 0:
            pl.semaphore_wait(barrier, has_left.astype(jnp.int32) + has_right.astype(jnp.int32))
        exchange(0, h, enc_leave.at[h, 0], enc_leave.at[h, 1])

    static_t = jnp.concatenate([static[...], jnp.zeros((5, nodes), F32)], axis=0).T
    total = static_t[:, 0:1] * mesh_embed[0:1, :]
    for f in range(1, static.shape[0]):
        total = total + static_t[:, f:f + 1] * mesh_embed[f:f + 1, :]
    mesh_state = silu(total)
    mesh_low = mesh_state.astype(BF)
    target = product(mesh_low, weight("et")).astype(BF)
    lane = lax.broadcasted_iota(jnp.int32, (1, LANES), 1)
    sel = {}
    for o in (1, 0, 2):
        live = lane < enc_counts[0, o]
        sel[o] = hot_rows(jnp.where(live, id_rows[base_er + o:base_er + o + 1, :], -1.0), nodes)
        joined = product(hot_columns(column(base_er + o), nodes), target)
        if o != 1:
            pre_enc[o // 2] = joined
    sel_side = jnp.concatenate([sel[0], sel[2]], axis=1)
    summed_own = []
    for h in range(2):
        rows = product(hot_own, grid_source[h]).astype(BF).astype(F32)
        own_hidden = silu(rows + product(hot_columns(column(base_er + 1), nodes), target[:, cols[h]]))
        summed_own.append(product(sel[1], own_hidden.astype(BF)))

    def join_weights(name_message, name_absorb):
        return product(weight(name_message), weight(name_absorb)).astype(BF)

    message_absorb = join_weights("em", "ea")
    acc = product(mesh_low, weight("er"))

    hot_halo = hot_columns(column(base_h), nodes)
    for j in range(blocks_m):
        at = slice(j * LANES, (j + 1) * LANES)
        ids = column(base_ms + j)
        hot_mesh[at, 0:rim_w] = hot_columns(ids, rim_w)
        hot_mesh[at, rim_w:2 * rim_w] = hot_columns(ids, rim_w, rim_w + nodes)
        hot_mesh[at, 2 * rim_w:ext_w] = hot_columns(ids, nodes, rim_w)
        hot_mesh[at, ext_w:ext_w + nodes] = hot_columns(column(base_mr + j), nodes)
        sel_mesh[:, at] = hot_rows(id_rows[base_mr + j:base_mr + j + 1, :], nodes)
    for o in range(3):
        place = (0, 2, 1)[o]
        for b in range(blocks_d):
            j = o * blocks_d + b
            at = slice(place * width_d + b * LANES, place * width_d + (b + 1) * LANES)
            hot_dec[at, 0:nodes] = hot_columns(column(base_ds + j), nodes)
            hot_dec[at, nodes:nodes + cells] = hot_columns(column(base_dr + j), cells)
            live = lane + b * LANES < dec_counts[0, o]
            row = jnp.where(live, id_rows[base_dr + j:base_dr + j + 1, :], -1.0)
            sel_dec[:, at] = hot_rows(row, cells)

    for h in range(2):
        arrive(0, h)
        for side in range(2):
            joined = enc_table[h, side].astype(F32) + pre_enc[side, :, cols[h]]
            hidden[h, side * width_e:(side + 1) * width_e, :] = silu(joined).astype(BF)
        summed = summed_own[h] + product(sel_side, hidden[h, 0:2 * width_e, :])
        acc = acc + product(summed.astype(BF), message_absorb[cols[h], :])
    mesh_state = mesh_state + norm_rows(product(silu(acc).astype(BF), weight("ef")))

    chunk = 512
    edges = blocks_m * LANES
    for l in range(layers):
        tag = str(l)
        mesh_low = mesh_state.astype(BF)
        w = weight("ps" + tag)
        for h in range(2):
            source = product(mesh_low, w[:, cols[h]]).astype(BF)
            rim[l, h] = product(hot_halo, source).astype(BF)
            exchange(1 + l, h, rim.at[l, h], rim.at[l, h])
            own_table[h, 0:nodes, :] = source
        w = weight("pt" + tag)
        for h in range(2):
            own_table[h, nodes:2 * nodes, :] = product(mesh_low, w[:, cols[h]]).astype(BF)
        for h in range(2):
            for c in range(edges // chunk):
                at = slice(c * chunk, (c + 1) * chunk)
                pre_mesh[h, at, :] = product(hot_mesh[at, 2 * rim_w:], own_table[h])
        acc = product(mesh_low, weight("pr" + tag))
        if l == 0:
            grid_tgt[...] = product(latent, weight("dt")).astype(BF)
            grid_kept = product(latent, weight("dr"))
        if l == layers - 1:
            for h in range(2):
                pre_dec[h] = product(hot_dec[:, nodes:], grid_tgt[:, cols[h]])
            message_absorb = join_weights("dm", "da")
        w = weight("pa" + tag)
        for h in range(2):
            arrive(1 + l, h)
            for c in range(edges // chunk):
                at = slice(c * chunk, (c + 1) * chunk)
                joined = pre_mesh[h, at, :] + product(hot_mesh[at, 0:2 * rim_w], rim_table[l, h])
                hidden[h, at, :] = silu(joined).astype(BF)
            summed = product(sel_mesh[...], hidden[h]).astype(BF)
            acc = acc + product(summed, w[cols[h], :])
        mesh_state = mesh_state + norm_rows(product(silu(acc).astype(BF), weight("pf" + tag)))

    mesh_low = mesh_state.astype(BF)
    w = weight("ds")
    for h in range(2):
        own_table[h, 0:nodes, :] = product(mesh_low, w[:, cols[h]]).astype(BF)
        exchange(1 + layers, h, own_table.at[h, pl.ds(0, nodes)], own_table.at[h, pl.ds(0, nodes)])

    def decode(h, place, table):
        at = slice(place * width_d, (place + 1) * width_d)
        joined = pre_dec[h, at, :] + product(hot_dec[at, 0:nodes], table)
        hidden[h, at, :] = silu(joined).astype(BF)

    summed_own = []
    for h in range(2):
        decode(h, 2, own_table[h, 0:nodes, :])
        summed_own.append(product(sel_dec[:, 2 * width_d:], hidden[h, 2 * width_d:3 * width_d, :]))
    acc = grid_kept
    for h in range(2):
        arrive(1 + layers, h)
        decode(h, 0, dec_table[h, 0])
        decode(h, 1, dec_table[h, 1])
        summed = summed_own[h] + product(sel_dec[:, 0:2 * width_d], hidden[h, 0:2 * width_d, :])
        acc = acc + product(summed.astype(BF), message_absorb[cols[h], :])
    out[...] = product_nt(readout_t[...], silu(acc).astype(BF)).astype(BF)

    for one, two in sent.values():
        @pl.when(has_left)
        def _(one=one):
            one.wait_send()

        @pl.when(has_right)
        def _(two=two):
            two.wait_send()


def body(
    n,
    grid_state,
    mesh_static,
    encoder_senders,
    encoder_receivers,
    encoder_counts,
    mesh_senders,
    mesh_receivers,
    halo_rows,
    backward_icosa_emitters,
    backward_cell_destination,
    backward_active_slot_amounts,
    grid_embed,
    mesh_embed,
    encoder_source,
    encoder_target,
    encoder_message,
    encoder_retain,
    encoder_absorb,
    encoder_finish,
    process_source,
    process_target,
    process_retain,
    process_absorb,
    process_finish,
    decoder_source,
    decoder_target,
    decoder_message,
    decoder_retain,
    decoder_absorb,
    readout_matrix,
):
    cells = grid_state.shape[0]
    nodes = mesh_static.shape[1]
    dim = grid_embed.shape[1]
    layers = process_source.shape[0]
    rim_w = halo_rows.shape[1]
    edges = mesh_senders.size
    width_e = encoder_senders.size // 3
    width_d = backward_icosa_emitters.size // 3
    n_weights = 11 + 5 * layers
    rounds = 2 + layers
    half = dim // 2
    vmem = pl.BlockSpec(memory_space=pltpu.VMEM)
    smem = pl.BlockSpec(memory_space=pltpu.SMEM)
    far = pl.BlockSpec(memory_space=pl.ANY)
    out_t = pl.pallas_call(
        functools.partial(kernel, n),
        out_shape=jax.ShapeDtypeStruct((readout_matrix.shape[1], cells), BF),
        in_specs=[vmem] * 4 + [smem] + [vmem] * 5 + [smem] + [vmem] * 3 + [far] * 16,
        out_specs=vmem,
        scratch_shapes=[
            pltpu.VMEM((n_weights, dim, dim), BF),
            pltpu.VMEM((LANES, LANES), F32),
            pltpu.VMEM((LANES, LANES), F32),
            pltpu.VMEM((2, 2, width_e, half), BF),
            pltpu.VMEM((2, 2, width_e, half), BF),
            pltpu.VMEM((2, width_e, dim), F32),
            pltpu.VMEM((layers, 2, rim_w, half), BF),
            pltpu.VMEM((layers, 2, 2 * rim_w, half), BF),
            pltpu.VMEM((2, 2 * nodes, half), BF),
            pltpu.VMEM((2, edges, half), F32),
            pltpu.VMEM((2, 2, nodes, half), BF),
            pltpu.VMEM((2, 3 * width_d, half), F32),
            pltpu.VMEM((cells, dim), BF),
            pltpu.VMEM((edges, 2 * rim_w + 2 * nodes), BF),
            pltpu.VMEM((nodes, edges), BF),
            pltpu.VMEM((3 * width_d, nodes + cells), BF),
            pltpu.VMEM((cells, 3 * width_d), BF),
            pltpu.VMEM((2, edges, half), BF),
            pltpu.SemaphoreType.DMA((n_weights,)),
            pltpu.SemaphoreType.DMA((4 * rounds,)),
            pltpu.SemaphoreType.DMA((4 * rounds,)),
        ],
        compiler_params=pltpu.CompilerParams(
            collective_id=0, has_side_effects=True, vmem_limit_bytes=56 * 1024 * 1024
        ),
    )(
        grid_state.T,
        mesh_static,
        encoder_senders,
        encoder_receivers,
        encoder_counts,
        mesh_senders,
        mesh_receivers,
        halo_rows,
        backward_icosa_emitters,
        backward_cell_destination,
        backward_active_slot_amounts,
        grid_embed,
        mesh_embed,
        readout_matrix.T,
        encoder_source,
        encoder_target,
        encoder_message,
        encoder_retain,
        encoder_absorb,
        encoder_finish,
        process_source,
        process_target,
        process_retain,
        process_absorb,
        process_finish,
        decoder_source,
        decoder_target,
        decoder_message,
        decoder_retain,
        decoder_absorb,
    )
    return out_t.T


def solution(mesh):
    placed = (
        P(("groups", "band"), None),
        P(None, "band"),
        P("band", None, None, None),
        P("band", None, None, None),
        P("band", None),
        P("band", None),
        P("band", None),
        P("band", None),
        P("band", None, None, None),
        P("band", None, None, None),
        P("band", None),
    ) + (P(),) * 19
    return jax.shard_map(
        functools.partial(body, mesh.shape["band"]),
        mesh=mesh,
        in_specs=placed,
        out_specs=P(("groups", "band"), None),
        check_vma=False,
    )
```

```python
import functools

import jax
import jax.numpy as jnp
from jax import lax
from jax.experimental import pallas as pl
from jax.experimental.pallas import tpu as pltpu
from jax.sharding import PartitionSpec as P

MESH = pl.DeviceIdType.MESH
BF = jnp.bfloat16
F32 = jnp.float32
LANES = 128


def product(left, right):
    return jnp.dot(left, right, preferred_element_type=F32)


def product_nt(left, right):
    return lax.dot_general(left, right, (((1,), (1,)), ((), ())), preferred_element_type=F32)


def product_tn(left, right):
    return lax.dot_general(left, right, (((0,), (0,)), ((), ())), preferred_element_type=F32)


def silu(x):
    half = 0.5 * x
    return half + half * jnp.tanh(half)


def norm_rows(values):
    centre = values - jnp.mean(values, axis=-1, keepdims=True)
    spread = jnp.mean(centre * centre, axis=-1, keepdims=True)
    return centre * lax.rsqrt(spread + 1e-05)


def hot_columns(column, width, first=0):
    ids = (lax.broadcasted_iota(jnp.int32, (column.shape[0], width), 1) + first).astype(F32)
    return jnp.where(column == ids, 1.0, 0.0).astype(BF)


def hot_rows(row, height):
    ids = lax.broadcasted_iota(jnp.int32, (height, row.shape[1]), 0).astype(F32)
    return jnp.where(row == ids, 1.0, 0.0).astype(BF)


def kernel(
    n,
    state_t,
    static,
    enc_send,
    enc_recv,
    enc_counts,
    mesh_send,
    mesh_recv,
    halo,
    dec_send,
    dec_recv,
    dec_counts,
    grid_embed,
    mesh_embed,
    readout_t,
    w_es,
    w_et,
    w_em,
    w_er,
    w_ea,
    w_ef,
    w_ps,
    w_pt,
    w_pr,
    w_pa,
    w_pf,
    w_ds,
    w_dt,
    w_dm,
    w_dr,
    w_da,
    out,
    weights,
    id_rows,
    id_cols,
    enc_leave,
    enc_table,
    pre_enc,
    rim,
    rim_table,
    own_table,
    pre_mesh,
    dec_table,
    pre_dec,
    grid_tgt,
    hot_mesh,
    sel_mesh,
    hot_dec,
    sel_dec,
    hidden,
    weight_sem,
    send_sem,
    recv_sem,
):
    layers = w_ps.shape[0]
    nodes = static.shape[1]
    cells = state_t.shape[1]
    width_e = enc_send.shape[2] * LANES
    blocks_d = dec_send.shape[2]
    width_d = blocks_d * LANES
    rim_w = halo.shape[1]
    blocks_m = mesh_send.shape[0]
    ext_w = nodes + 2 * rim_w

    me = lax.axis_index("band")
    left = lax.rem(me + n - 1, n)
    right = lax.rem(me + 1, n)
    has_left = me > 0
    has_right = me < n - 1

    barrier = pltpu.get_barrier_semaphore()

    @pl.when(has_left)
    def _():
        pl.semaphore_signal(barrier, inc=1, device_id={"band": left}, device_id_type=MESH)

    @pl.when(has_right)
    def _():
        pl.semaphore_signal(barrier, inc=1, device_id={"band": right}, device_id_type=MESH)

    order = [w_es, w_et, w_em, w_ea, w_er, w_ef]
    names = ["es", "et", "em", "ea", "er", "ef"]
    for l in range(layers):
        order += [w.at[l] for w in (w_ps, w_pt, w_pr, w_pa, w_pf)]
        names += [a + str(l) for a in ("ps", "pt", "pr", "pa", "pf")]
    order += [w_ds, w_dt, w_dr, w_dm, w_da]
    names += ["ds", "dt", "dr", "dm", "da"]
    copies = {}
    for k, (name, ref) in enumerate(zip(names, order)):
        copy = pltpu.make_async_copy(ref, weights.at[k], weight_sem.at[k])
        copy.start()
        copies[name] = (copy, k)

    def weight(name):
        copy, k = copies[name]
        copy.wait()
        return weights[k]

    dim = weights.shape[-1]
    half = dim // 2
    cols = [slice(0, half), slice(half, dim)]

    def to_side(k, src, dst, side):
        return pltpu.make_async_remote_copy(
            src_ref=src, dst_ref=dst, send_sem=send_sem.at[k], recv_sem=recv_sem.at[k],
            device_id={"band": side}, device_id_type=MESH)

    lows, highs = {}, {}
    for h in range(2):
        lows[0, h], highs[0, h] = enc_table.at[h, 0], enc_table.at[h, 1]
        for l in range(layers):
            lows[1 + l, h] = rim_table.at[l, h, pl.ds(0, rim_w)]
            highs[1 + l, h] = rim_table.at[l, h, pl.ds(rim_w, rim_w)]
        for g in range(2):
            part = pl.ds(g * (nodes // 2), nodes // 2)
            lows[1 + layers + g, h] = dec_table.at[h, 0, part]
            highs[1 + layers + g, h] = dec_table.at[h, 1, part]

    sent = {}

    def exchange(r, h, src_left, src_right):
        k = 2 * (2 * r + h)
        one = to_side(k, src_left, highs[r, h], left)
        two = to_side(k + 1, src_right, lows[r, h], right)

        @pl.when(has_left)
        def _():
            one.start()

        @pl.when(has_right)
        def _():
            two.start()

        sent[r, h] = (one, two)

    def arrive(r, h):
        one, two = sent[r, h]

        @pl.when(has_left)
        def _():
            two.wait_recv()

        @pl.when(has_right)
        def _():
            one.wait_recv()

    @pl.when(jnp.logical_not(has_left))
    def _():
        for ref in lows.values():
            ref[...] = jnp.zeros(ref.shape, BF)

    @pl.when(jnp.logical_not(has_right))
    def _():
        for ref in highs.values():
            ref[...] = jnp.zeros(ref.shape, BF)

    id_rows[...] = jnp.zeros(id_rows.shape, F32)
    base_ms, base_mr = 0, blocks_m
    base_h = 2 * blocks_m
    base_es = base_h + 8
    base_er = base_es + 8
    base_ds = base_er + 8
    base_dr = base_ds + 8
    id_rows[base_ms:base_ms + blocks_m, :] = mesh_send[...].astype(F32)
    id_rows[base_mr:base_mr + blocks_m, :] = mesh_recv[...].astype(F32)
    id_rows[base_h:base_h + 1, :] = halo[...].astype(F32)
    for o in range(3):
        id_rows[base_es + o:base_es + o + 1, :] = enc_send[0, o].astype(F32)
        id_rows[base_er + o:base_er + o + 1, :] = enc_recv[0, o].astype(F32)
        id_rows[base_ds + 2 * o:base_ds + 2 * o + 2, :] = dec_send[0, o].astype(F32)
        id_rows[base_dr + 2 * o:base_dr + 2 * o + 2, :] = dec_recv[0, o].astype(F32)
    id_cols[...] = id_rows[...].T

    def column(j):
        return id_cols[:, j:j + 1]

    latent = norm_rows(silu(product_tn(state_t[...], grid_embed[...]))).astype(BF)
    w = weight("es")
    hot_left = hot_columns(column(base_es), cells)
    hot_right = hot_columns(column(base_es + 2), cells)
    hot_own = hot_columns(column(base_es + 1), cells)
    grid_source = []
    for h in range(2):
        grid_source.append(product(latent, w[:, cols[h]]).astype(BF))
        enc_leave[h, 0] = product(hot_left, grid_source[h]).astype(BF)
        enc_leave[h, 1] = product(hot_right, grid_source[h]).astype(BF)
        if h == 0:
            pl.semaphore_wait(barrier, has_left.astype(jnp.int32) + has_right.astype(jnp.int32))
        exchange(0, h, enc_leave.at[h, 0], enc_leave.at[h, 1])

    static_t = jnp.concatenate([static[...], jnp.zeros((5, nodes), F32)], axis=0).T
    total = static_t[:, 0:1] * mesh_embed[0:1, :]
    for f in range(1, static.shape[0]):
        total = total + static_t[:, f:f + 1] * mesh_embed[f:f + 1, :]
    mesh_state = silu(total)
    mesh_low = mesh_state.astype(BF)
    target = product(mesh_low, weight("et")).astype(BF)
    lane = lax.broadcasted_iota(jnp.int32, (1, LANES), 1)
    sel = {}
    for o in (1, 0, 2):
        live = lane < enc_counts[0, o]
        sel[o] = hot_rows(jnp.where(live, id_rows[base_er + o:base_er + o + 1, :], -1.0), nodes)
        joined = product(hot_columns(column(base_er + o), nodes), target)
        if o != 1:
            pre_enc[o // 2] = joined
    sel_side = jnp.concatenate([sel[0], sel[2]], axis=1)
    summed_own = []
    for h in range(2):
        rows = product(hot_own, grid_source[h]).astype(BF).astype(F32)
        own_hidden = silu(rows + product(hot_columns(column(base_er + 1), nodes), target[:, cols[h]]))
        summed_own.append(product(sel[1], own_hidden.astype(BF)))

    def join_weights(name_message, name_absorb):
        return product(weight(name_message), weight(name_absorb)).astype(BF)

    message_absorb = join_weights("em", "ea")
    acc = product(mesh_low, weight("er"))

    hot_halo = hot_columns(column(base_h), nodes)
    for j in range(blocks_m):
        at = slice(j * LANES, (j + 1) * LANES)
        ids = column(base_ms + j)
        hot_mesh[at, 0:rim_w] = hot_columns(ids, rim_w)
        hot_mesh[at, rim_w:2 * rim_w] = hot_columns(ids, rim_w, rim_w + nodes)
        hot_mesh[at, 2 * rim_w:ext_w] = hot_columns(ids, nodes, rim_w)
        hot_mesh[at, ext_w:ext_w + nodes] = hot_columns(column(base_mr + j), nodes)
        sel_mesh[:, at] = hot_rows(id_rows[base_mr + j:base_mr + j + 1, :], nodes)
    for o in range(3):
        place = (0, 2, 1)[o]
        for b in range(blocks_d):
            j = o * blocks_d + b
            at = slice(place * width_d + b * LANES, place * width_d + (b + 1) * LANES)
            hot_dec[at, 0:nodes] = hot_columns(column(base_ds + j), nodes)
            hot_dec[at, nodes:nodes + cells] = hot_columns(column(base_dr + j), cells)
            live = lane + b * LANES < dec_counts[0, o]
            row = jnp.where(live, id_rows[base_dr + j:base_dr + j + 1, :], -1.0)
            sel_dec[:, at] = hot_rows(row, cells)

    for h in range(2):
        arrive(0, h)
        for side in range(2):
            joined = enc_table[h, side].astype(F32) + pre_enc[side, :, cols[h]]
            hidden[h, side * width_e:(side + 1) * width_e, :] = silu(joined).astype(BF)
        summed = summed_own[h] + product(sel_side, hidden[h, 0:2 * width_e, :])
        acc = acc + product(summed.astype(BF), message_absorb[cols[h], :])
    mesh_state = mesh_state + norm_rows(product(silu(acc).astype(BF), weight("ef")))

    chunk = 512
    edges = blocks_m * LANES
    for l in range(layers):
        tag = str(l)
        mesh_low = mesh_state.astype(BF)
        w = weight("ps" + tag)
        for h in range(2):
            source = product(mesh_low, w[:, cols[h]]).astype(BF)
            rim[l, h] = product(hot_halo, source).astype(BF)
            exchange(1 + l, h, rim.at[l, h], rim.at[l, h])
            own_table[h, 0:nodes, :] = source
        w = weight("pt" + tag)
        for h in range(2):
            own_table[h, nodes:2 * nodes, :] = product(mesh_low, w[:, cols[h]]).astype(BF)
        for h in range(2):
            for c in range(edges // chunk):
                at = slice(c * chunk, (c + 1) * chunk)
                pre_mesh[h, at, :] = product(hot_mesh[at, 2 * rim_w:], own_table[h])
        acc = product(mesh_low, weight("pr" + tag))
        if l == 0:
            grid_tgt[...] = product(latent, weight("dt")).astype(BF)
            grid_kept = product(latent, weight("dr"))
        if l == layers - 1:
            for h in range(2):
                pre_dec[h] = product(hot_dec[:, nodes:], grid_tgt[:, cols[h]])
            message_absorb = join_weights("dm", "da")
        w = weight("pa" + tag)
        for h in range(2):
            arrive(1 + l, h)
            for c in range(edges // chunk):
                at = slice(c * chunk, (c + 1) * chunk)
                joined = pre_mesh[h, at, :] + product(hot_mesh[at, 0:2 * rim_w], rim_table[l, h])
                hidden[h, at, :] = silu(joined).astype(BF)
            summed = product(sel_mesh[...], hidden[h]).astype(BF)
            acc = acc + product(summed, w[cols[h], :])
        if l < layers - 1:
            mesh_state = mesh_state + norm_rows(product(silu(acc).astype(BF), weight("pf" + tag)))

    w_finish = weight("pf" + str(layers - 1))
    w = weight("ds")
    for g in range(2):
        first = g * (nodes // 2)
        at = slice(first, first + nodes // 2)
        inner = silu(acc[at]).astype(BF)
        mesh_low = (mesh_state[at] + norm_rows(product(inner, w_finish))).astype(BF)
        for h in range(2):
            own_table[h, at, :] = product(mesh_low, w[:, cols[h]]).astype(BF)
            part = own_table.at[h, pl.ds(first, nodes // 2)]
            exchange(1 + layers + g, h, part, part)

    def decode(h, place, table):
        at = slice(place * width_d, (place + 1) * width_d)
        joined = pre_dec[h, at, :] + product(hot_dec[at, 0:nodes], table)
        hidden[h, at, :] = silu(joined).astype(BF)

    summed_own = []
    for h in range(2):
        decode(h, 2, own_table[h, 0:nodes, :])
        summed_own.append(product(sel_dec[:, 2 * width_d:], hidden[h, 2 * width_d:3 * width_d, :]))
    acc = grid_kept
    for h in range(2):
        arrive(1 + layers, h)
        arrive(2 + layers, h)
        decode(h, 0, dec_table[h, 0])
        decode(h, 1, dec_table[h, 1])
        summed = summed_own[h] + product(sel_dec[:, 0:2 * width_d], hidden[h, 0:2 * width_d, :])
        acc = acc + product(summed.astype(BF), message_absorb[cols[h], :])
    out[...] = product_nt(readout_t[...], silu(acc).astype(BF)).astype(BF)

    for one, two in sent.values():
        @pl.when(has_left)
        def _(one=one):
            one.wait_send()

        @pl.when(has_right)
        def _(two=two):
            two.wait_send()


def body(
    n,
    grid_state,
    mesh_static,
    encoder_senders,
    encoder_receivers,
    encoder_counts,
    mesh_senders,
    mesh_receivers,
    halo_rows,
    backward_icosa_emitters,
    backward_cell_destination,
    backward_active_slot_amounts,
    grid_embed,
    mesh_embed,
    encoder_source,
    encoder_target,
    encoder_message,
    encoder_retain,
    encoder_absorb,
    encoder_finish,
    process_source,
    process_target,
    process_retain,
    process_absorb,
    process_finish,
    decoder_source,
    decoder_target,
    decoder_message,
    decoder_retain,
    decoder_absorb,
    readout_matrix,
):
    cells = grid_state.shape[0]
    nodes = mesh_static.shape[1]
    dim = grid_embed.shape[1]
    layers = process_source.shape[0]
    rim_w = halo_rows.shape[1]
    edges = mesh_senders.size
    width_e = encoder_senders.size // 3
    width_d = backward_icosa_emitters.size // 3
    n_weights = 11 + 5 * layers
    rounds = 3 + layers
    half = dim // 2
    vmem = pl.BlockSpec(memory_space=pltpu.VMEM)
    smem = pl.BlockSpec(memory_space=pltpu.SMEM)
    far = pl.BlockSpec(memory_space=pl.ANY)
    out_t = pl.pallas_call(
        functools.partial(kernel, n),
        out_shape=jax.ShapeDtypeStruct((readout_matrix.shape[1], cells), BF),
        in_specs=[vmem] * 4 + [smem] + [vmem] * 5 + [smem] + [vmem] * 3 + [far] * 16,
        out_specs=vmem,
        scratch_shapes=[
            pltpu.VMEM((n_weights, dim, dim), BF),
            pltpu.VMEM((LANES, LANES), F32),
            pltpu.VMEM((LANES, LANES), F32),
            pltpu.VMEM((2, 2, width_e, half), BF),
            pltpu.VMEM((2, 2, width_e, half), BF),
            pltpu.VMEM((2, width_e, dim), F32),
            pltpu.VMEM((layers, 2, rim_w, half), BF),
            pltpu.VMEM((layers, 2, 2 * rim_w, half), BF),
            pltpu.VMEM((2, 2 * nodes, half), BF),
            pltpu.VMEM((2, edges, half), F32),
            pltpu.VMEM((2, 2, nodes, half), BF),
            pltpu.VMEM((2, 3 * width_d, half), F32),
            pltpu.VMEM((cells, dim), BF),
            pltpu.VMEM((edges, 2 * rim_w + 2 * nodes), BF),
            pltpu.VMEM((nodes, edges), BF),
            pltpu.VMEM((3 * width_d, nodes + cells), BF),
            pltpu.VMEM((cells, 3 * width_d), BF),
            pltpu.VMEM((2, edges, half), BF),
            pltpu.SemaphoreType.DMA((n_weights,)),
            pltpu.SemaphoreType.DMA((4 * rounds,)),
            pltpu.SemaphoreType.DMA((4 * rounds,)),
        ],
        compiler_params=pltpu.CompilerParams(
            collective_id=0, has_side_effects=True, vmem_limit_bytes=56 * 1024 * 1024
        ),
    )(
        grid_state.T,
        mesh_static,
        encoder_senders,
        encoder_receivers,
        encoder_counts,
        mesh_senders,
        mesh_receivers,
        halo_rows,
        backward_icosa_emitters,
        backward_cell_destination,
        backward_active_slot_amounts,
        grid_embed,
        mesh_embed,
        readout_matrix.T,
        encoder_source,
        encoder_target,
        encoder_message,
        encoder_retain,
        encoder_absorb,
        encoder_finish,
        process_source,
        process_target,
        process_retain,
        process_absorb,
        process_finish,
        decoder_source,
        decoder_target,
        decoder_message,
        decoder_retain,
        decoder_absorb,
    )
    return out_t.T


def solution(mesh):
    placed = (
        P(("groups", "band"), None),
        P(None, "band"),
        P("band", None, None, None),
        P("band", None, None, None),
        P("band", None),
        P("band", None),
        P("band", None),
        P("band", None),
        P("band", None, None, None),
        P("band", None, None, None),
        P("band", None),
    ) + (P(),) * 19
    return jax.shard_map(
        functools.partial(body, mesh.shape["band"]),
        mesh=mesh,
        in_specs=placed,
        out_specs=P(("groups", "band"), None),
        check_vma=False,
    )
```
